32 devices in a mesh: obs: 16 (over z, y, x), head: 2 (over core).
Axes of the slice: x: 2, y: 2, z: 4, core: 2. Of those that a mesh axis runs over, the one named last changes fastest.
Arguments:
- queries: bfloat16 [256, 2048], P('obs', 'head'), may hold values from -6 to 6
- out_grad: bfloat16 [256, 2048], P('obs', 'head'), may hold values from -6 to 6
- attn_out: bfloat16 [256, 2048], P('obs', 'head'), may hold values from -6 to 6
- logsumexp: float32 [256, 16], P('obs', 'head'), may hold values from 2.5 to 4.5
- keys: bfloat16 [6144, 2048], P('obs', 'head'), may hold values from -6 to 6
- values: bfloat16 [6144, 2048], P('obs', 'head'), may hold values from -6 to 6
- obs_counts: int32 [16], P('obs'), may hold values from 1 to 384, as said below
- query_weight: bfloat16 [2048, 2048], P(None, 'head'), may hold values from -0.125 to 0.125
Outputs:
- key_grad: bfloat16 [6144, 2048], P('obs', 'head')
- value_grad: bfloat16 [6144, 2048], P('obs', 'head')
- query_grad: bfloat16 [256, 2048], P('obs', 'head')
- grid_grad: bfloat16 [256, 2048], P('obs', 'head')
The draws below stay inside these ranges and needn't reach their ends.
Inputs may be any that keep to these rules, and one draw needn't show every extreme that they name: Each index of obs holds its tokens in its first obs_counts slots of 384; in every draw some index is full, with exactly 384.
All inputs are finite; a program needn't handle non-finite values.
Results may differ from the reference program's by a relative error of at most 0.0055.
Values may be sent and summed in bfloat16 or wider, within the bound.
No kernel may reach another device: no remote copies, remote signals or barrier semaphores. Data moves between devices by JAX's collectives and lax.ppermute only.
A program may use at most 64 MiB of HBM per device.

```python
import math
import jax
import jax.numpy as jnp
from jax import lax

D = 2048
H = 16
DH = 128
TOK_DEV = 384
Q = 256
NOBS = 6144
N_OBS = 16


def draw_obs_counts(key, part):
    key_level, key_jitter, key_full = jax.random.split(jax.random.fold_in(key, 17), 3)
    levels = jax.random.randint(key_level, (N_OBS,), 0, 4)
    base_counts = jnp.right_shift(jnp.full((N_OBS,), TOK_DEV, jnp.int32), levels.astype(jnp.int32))
    jitter = jax.random.randint(key_jitter, (N_OBS,), 0, base_counts // 4 + 1)
    full_index = jax.random.randint(key_full, (), 0, N_OBS)
    counts = jnp.where(jnp.arange(N_OBS, dtype=jnp.int32) == full_index, TOK_DEV, base_counts - jitter)
    return jnp.maximum(counts, 1).astype(jnp.int32)


def block_levels(rng, dims, cuts, smallest, largest):
    def one(dim, shards_of):
        heights = jax.random.uniform(jax.random.fold_in(jax.random.fold_in(rng, 6), dim), (shards_of,), jnp.float32, smallest / len(cuts), largest / len(cuts))
        return jnp.repeat(jnp.exp(heights), dims[dim] // shards_of).reshape((-1,) + (1,) * (len(dims) - dim - 1))

    level = one(*cuts[0])
    for cut in cuts[1:]:
        level = level * one(*cut)
    return level


def centred(key, shape, spread, most, pieces=(), kind=jnp.bfloat16):
    values = spread * jax.random.normal(key, shape, jnp.float32)
    if pieces:
        values = values * block_levels(key, shape, pieces, -0.22, 0.18)
    return jnp.clip(values, -most, most).astype(kind)


def setup_inputs(seed: int = 0) -> dict:
    seeds = jax.random.split(jax.random.key(seed), 9)
    return {
        "queries": centred(seeds[0], (Q, D), 1.0, 6.0, ((0, 16), (1, 2))),
        "out_grad": centred(seeds[1], (Q, D), 1.0, 6.0, ((0, 16), (1, 2))),
        "attn_out": centred(seeds[2], (Q, D), 1.0, 6.0, ((0, 16), (1, 2))),
        "logsumexp": jnp.clip(2.5 + 2.0 * jax.random.uniform(seeds[3], (Q, H), jnp.float32) ** block_levels(seeds[3], (Q, H), ((0, 16), (1, 2)), -0.2, 0.2), 2.5, 4.5),
        "keys": centred(seeds[4], (NOBS, D), 1.0, 6.0, ((0, 16), (1, 2))),
        "values": centred(seeds[5], (NOBS, D), 1.0, 6.0, ((0, 16), (1, 2))),
        "obs_counts": draw_obs_counts(jax.random.fold_in(seeds[8], 71), 0),
        "query_weight": centred(seeds[7], (D, D), D ** -0.5, 0.125, ((1, 2),)),
    }


def reference(queries, out_grad, attn_out, logsumexp, keys, values, obs_counts, query_weight):
    softmax_scale = 1.0 / math.sqrt(DH)
    query_heads = queries.reshape(Q, H, DH).transpose(1, 0, 2)
    grad_heads = out_grad.reshape(Q, H, DH).transpose(1, 0, 2)
    delta = lax.optimization_barrier(jnp.sum(out_grad.astype(jnp.float32).reshape(Q, H, DH) * attn_out.astype(jnp.float32).reshape(Q, H, DH), axis=2))
    key_heads = keys.reshape(N_OBS, TOK_DEV, H, DH).transpose(2, 0, 1, 3)
    value_heads = values.reshape(N_OBS, TOK_DEV, H, DH).transpose(2, 0, 1, 3)
    live = (jnp.arange(TOK_DEV, dtype=jnp.int32)[None, :] < obs_counts[:, None]).astype(jnp.float32)

    def one_head(inputs):
        query_now, grad_now, lse_now, delta_now, key_now, value_now = inputs

        def key_block(query_acc, blocks):
            key_rows, value_rows, live_rows = blocks
            scores = jnp.dot(query_now, key_rows.T, preferred_element_type=jnp.float32) * softmax_scale
            probs = jnp.exp(scores - lse_now[:, None]) * live_rows[None, :]
            value_part = jnp.dot(probs.astype(jnp.bfloat16).T, grad_now, preferred_element_type=jnp.float32)
            dprobs = jnp.dot(grad_now, value_rows.T, preferred_element_type=jnp.float32)
            dscores = (probs * (dprobs - delta_now[:, None])).astype(jnp.bfloat16)
            key_part = jnp.dot(dscores.T, query_now, preferred_element_type=jnp.float32) * softmax_scale
            query_acc = query_acc + jnp.dot(dscores, key_rows, preferred_element_type=jnp.float32) * softmax_scale
            return (query_acc, (key_part, value_part))
        query_acc, parts = lax.scan(key_block, jnp.zeros((Q, DH), jnp.float32), (key_now, value_now, live))
        return (query_acc, parts[0], parts[1])
    query_sum, key_part, value_part = lax.map(one_head, (query_heads, grad_heads, logsumexp.T, delta.T, key_heads, value_heads))
    key_grad = key_part.transpose(1, 2, 0, 3).reshape(NOBS, D).astype(jnp.bfloat16)
    value_grad = value_part.transpose(1, 2, 0, 3).reshape(NOBS, D).astype(jnp.bfloat16)
    query_grad = query_sum.transpose(1, 0, 2).reshape(Q, D).astype(jnp.bfloat16)
    grid_grad = jnp.dot(query_grad, query_weight.T, preferred_element_type=jnp.float32).astype(jnp.bfloat16)
    return (key_grad, value_grad, query_grad, grid_grad)
```

```python
import functools
import math

import jax
import jax.numpy as jnp
from jax import lax
from jax.experimental import pallas as pl
from jax.experimental.pallas import tpu as pltpu
from jax.sharding import PartitionSpec as P

DH = 128
LANES = 128
SCALE = 1.0 / math.sqrt(DH)
BF16 = jnp.bfloat16
F32 = jnp.float32


def dot(a, b, contract):
    return lax.dot_general(a, b, (contract, ((), ())), preferred_element_type=F32)


def call(body, out_shape, *args, flops=0, moved=0):
    vmem = pl.BlockSpec(memory_space=pltpu.VMEM)
    specs = [
        pl.BlockSpec(memory_space=pltpu.SMEM) if a.dtype == jnp.int32 else vmem for a in args
    ]
    return pl.pallas_call(
        body,
        out_shape=out_shape,
        in_specs=specs,
        out_specs=jax.tree.map(lambda _: vmem, out_shape),
        compiler_params=pltpu.CompilerParams(vmem_limit_bytes=40 * 2**20),
        cost_estimate=pl.CostEstimate(flops=flops, bytes_accessed=moved, transcendentals=0),
    )(*args)


def pack_body(heads, q_ref, g_ref, a_ref, lse_ref, out_ref):
    width = q_ref.shape[1]
    out_ref[:, :width] = q_ref[...]
    out_ref[:, width : 2 * width] = g_ref[...]
    meta = out_ref.shape[1] - 2 * width
    shape = (q_ref.shape[0], meta)
    lane = lax.broadcasted_iota(jnp.int32, shape, 1)
    slot = lax.rem(lane, 2 * heads)
    x = jnp.zeros(shape, F32)
    for h in range(heads):
        cols = slice(h * DH, (h + 1) * DH)
        delta = jnp.sum(g_ref[:, cols].astype(F32) * a_ref[:, cols].astype(F32), axis=1, keepdims=True)
        x = jnp.where(slot == h, lse_ref[:, h : h + 1], x)
        x = jnp.where(slot == heads + h, delta, x)
    high = x.astype(BF16).astype(F32)
    mid = (x - high).astype(BF16).astype(F32)
    low = x - high - mid
    term = lane // (2 * heads)
    out_ref[:, 2 * width :] = jnp.where(
        term == 0, high, jnp.where(term == 1, mid, jnp.where(term == 2, low, 0.0))
    ).astype(BF16)


def chunk_body(heads, count_ref, rows_ref, k_ref, v_ref, p_ref, ds_ref, qsum_ref):
    rows, tokens = rows_ref.shape[0], k_ref.shape[0]
    width = k_ref.shape[1]
    live = lax.broadcasted_iota(jnp.int32, (rows, tokens), 1) < count_ref[0]
    meta = rows_ref[:, 2 * width :].astype(F32)

    def whole(slot):
        cut = lambda t: meta[:, t * 2 * heads + slot : t * 2 * heads + slot + 1]
        return cut(0) + cut(1) + cut(2)

    for h in range(heads):
        cols = slice(h * DH, (h + 1) * DH)
        k = k_ref[:, cols]
        scores = dot(rows_ref[:, cols], k, ((1,), (1,))) * SCALE
        probs = jnp.where(live, jnp.exp(scores - whole(h)), 0.0)
        p_ref[h] = probs.astype(BF16)
        dprobs = dot(
            rows_ref[:, width + h * DH : width + (h + 1) * DH], v_ref[:, cols], ((1,), (1,))
        )
        ds = (probs * (dprobs - whole(heads + h))).astype(BF16)
        ds_ref[h] = ds
        qsum_ref[:, cols] = (dot(ds, k, ((1,), (0,))) * SCALE).astype(qsum_ref.dtype)


def chunk(heads, count, rows, keys, values, dtype):
    n, (tokens, width) = rows.shape[0], keys.shape
    return call(
        functools.partial(chunk_body, heads),
        (
            jax.ShapeDtypeStruct((heads, n, tokens), BF16),
            jax.ShapeDtypeStruct((heads, n, tokens), BF16),
            jax.ShapeDtypeStruct((n, width), dtype),
        ),
        count,
        rows,
        keys,
        values,
        flops=6 * heads * n * tokens * DH,
        moved=2 * keys.size * 2 + 4 * heads * n * tokens,
    )


def kv_body(heads, n, *refs):
    p_refs, ds_refs, row_refs = refs[:n], refs[n : 2 * n], refs[2 * n : 3 * n]
    dk_ref, dv_ref = refs[3 * n :]
    width = dk_ref.shape[1]
    for h in range(heads):
        cols = slice(h * DH, (h + 1) * DH)
        gcols = slice(width + h * DH, width + (h + 1) * DH)
        p = jnp.concatenate([r[h] for r in p_refs], axis=0)
        g = jnp.concatenate([r[:, gcols] for r in row_refs], axis=0)
        dv_ref[:, cols] = dot(p, g, ((0,), (0,))).astype(BF16)
        ds = jnp.concatenate([r[h] for r in ds_refs], axis=0)
        q = jnp.concatenate([r[:, cols] for r in row_refs], axis=0)
        dk_ref[:, cols] = (dot(ds, q, ((0,), (0,))) * SCALE).astype(BF16)


def gather_sum_body(n, *refs):
    mine, others, keep, outs = refs[0], refs[1:n], refs[n], refs[n + 1 :]
    total = mine[...]
    for r in others:
        total = total + r[...].astype(F32)
    rows = keep.shape[0]
    keep[...] = total[:rows]
    for i, out in enumerate(outs):
        out[...] = total[(i + 1) * rows : (i + 2) * rows].astype(BF16)


def last_sum_body(*refs):
    total = refs[0][...]
    for r in refs[1:-1]:
        total = total + r[...].astype(F32)
    refs[-1][...] = total.astype(BF16)


def grid_body(q_ref, w_ref, out_ref):
    out_ref[...] = dot(q_ref[...], w_ref[...], ((1,), (1,)))


def shifted(i, k, n):
    return i ^ k if n & (n - 1) == 0 else (i + k) % n


def send(x, high, low, k_high, k_low, back=False):
    pairs = []
    for a in range(high):
        for b in range(low):
            there = shifted(a, k_high, high) * low + shifted(b, k_low, low)
            pairs.append((there, a * low + b) if back else (a * low + b, there))
    return lax.ppermute(x, "obs", pairs)


def on_device(obs, head, queries, out_grad, attn_out, logsumexp, keys, values, obs_counts, query_weight):
    own, width = queries.shape
    heads = width // DH
    tokens = keys.shape[0]
    low = 4 if obs % 4 == 0 else obs
    high = obs // low
    meta = -(-6 * heads // LANES) * LANES

    packed = call(
        functools.partial(pack_body, heads),
        jax.ShapeDtypeStruct((own, 2 * width + meta), BF16),
        queries,
        out_grad,
        attn_out,
        logsumexp,
    )
    column = [packed] + [send(packed, high, low, k, 0) for k in range(1, high)]
    column = jnp.concatenate(column, axis=0)
    chunks = [column] + [send(column, high, low, 0, k) for k in range(1, low)]

    probs, dscores, parts = [], [], []
    for i, rows in enumerate(chunks):
        p, ds, part = chunk(heads, obs_counts, rows, keys, values, BF16 if i else F32)
        probs.append(p)
        dscores.append(ds)
        parts.append(send(part, high, low, 0, i, back=True) if i else part)

    sums = call(
        functools.partial(gather_sum_body, low),
        (jax.ShapeDtypeStruct((own, width), F32),)
        + (jax.ShapeDtypeStruct((own, width), BF16),) * (high - 1),
        *parts,
    )
    received = [send(s, high, low, k + 1, 0, back=True) for k, s in enumerate(sums[1:])]

    key_grad, value_grad = call(
        functools.partial(kv_body, heads, low),
        (jax.ShapeDtypeStruct((tokens, width), BF16),) * 2,
        *probs,
        *dscores,
        *chunks,
        flops=4 * heads * low * high * own * tokens * DH,
        moved=4 * heads * low * high * own * tokens + 4 * tokens * width,
    )
    query_grad = call(
        last_sum_body, jax.ShapeDtypeStruct((own, width), BF16), sums[0], *received
    )
    partial = call(
        grid_body,
        jax.ShapeDtypeStruct((own, query_weight.shape[0]), F32),
        query_grad,
        query_weight,
        flops=2 * own * query_weight.size,
        moved=2 * query_weight.size,
    )
    if head == 2:
        me = lax.axis_index("head")
        mine = lax.dynamic_slice_in_dim(partial, me * width, width, 1)
        other = lax.dynamic_slice_in_dim(partial, (1 - me) * width, width, 1)
        grid = mine + lax.ppermute(other, "head", [(0, 1), (1, 0)])
    else:
        grid = lax.psum_scatter(partial, "head", scatter_dimension=1, tiled=True)
    return key_grad, value_grad, query_grad, grid.astype(BF16)


def solution(mesh):
    both = P("obs", "head")
    return jax.shard_map(
        functools.partial(on_device, mesh.shape["obs"], mesh.shape["head"]),
        mesh=mesh,
        in_specs=(both, both, both, both, both, both, P("obs"), P(None, "head")),
        out_specs=(both,) * 4,
        check_vma=False,
    )
```

```python
import functools
import math

import jax
import jax.numpy as jnp
from jax import lax
from jax.experimental import pallas as pl
from jax.experimental.pallas import tpu as pltpu
from jax.sharding import PartitionSpec as P

DH = 128
LANES = 128
SCALE = 1.0 / math.sqrt(DH)
BF16 = jnp.bfloat16
F32 = jnp.float32


def dot(a, b, contract):
    return lax.dot_general(a, b, (contract, ((), ())), preferred_element_type=F32)


def call(body, out_shape, *args, hbm=(), after=None, scratch=(), flops=0, moved=0):
    vmem = pl.BlockSpec(memory_space=pltpu.VMEM)
    specs = [
        pl.BlockSpec(memory_space=pltpu.SMEM)
        if a.dtype == jnp.int32
        else pl.BlockSpec(memory_space=pl.ANY) if i in hbm else vmem
        for i, a in enumerate(args)
    ]
    args = [
        a
        if a.dtype == jnp.int32
        else pltpu.with_memory_space_constraint(a, pltpu.HBM if i in hbm else pltpu.VMEM)
        for i, a in enumerate(args)
    ]
    n = len(args)
    if after is not None:
        args.append(
            pltpu.with_memory_space_constraint(after[0], pltpu.HBM)
            if isinstance(after, list)
            else pltpu.with_memory_space_constraint(after, pltpu.VMEM)
        )
        specs.append(pl.BlockSpec(memory_space=pl.ANY))
    return pl.pallas_call(
        (lambda *refs: body(*refs[:n], *refs[n + 1 :])) if after is not None else body,
        out_shape=out_shape,
        in_specs=specs,
        out_specs=jax.tree.map(lambda _: vmem, out_shape, is_leaf=lambda x: hasattr(x, "shape")),
        scratch_shapes=scratch,
        compiler_params=pltpu.CompilerParams(vmem_limit_bytes=14 * 2**20),
        cost_estimate=pl.CostEstimate(flops=flops, bytes_accessed=moved, transcendentals=0),
    )(*args)


def shape(*sizes, dtype=BF16):
    return jax.ShapeDtypeStruct(sizes, dtype)


def local(*sizes, dtype=BF16):
    return pltpu.VMEM(sizes, dtype)


def pack_body(heads, q_hbm, g_hbm, a_hbm, lse_hbm, out_ref, a_ref, lse_ref, sems):
    rows, width = a_ref.shape
    copies = [
        pltpu.make_async_copy(src, dst, sems.at[i])
        for i, (src, dst) in enumerate(
            (
                (g_hbm, out_ref.at[:, width : 2 * width]),
                (a_hbm, a_ref),
                (lse_hbm, lse_ref),
                (q_hbm, out_ref.at[:, :width]),
            )
        )
    ]
    for c in copies:
        c.start()
    meta = out_ref.shape[1] - 2 * width
    lane = lax.broadcasted_iota(jnp.int32, (rows, meta), 1)
    slot = lax.rem(lane, 2 * heads)
    term = lane // (2 * heads)
    diagonal = lax.broadcasted_iota(jnp.int32, (rows, rows), 0) == lax.broadcasted_iota(
        jnp.int32, (rows, rows), 1
    )
    x = jnp.zeros((rows, meta), F32)
    for c in copies[:3]:
        c.wait()
    for h in range(heads):
        product = out_ref[:, width + h * DH : width + (h + 1) * DH].astype(F32) * a_ref[
            :, h * DH : (h + 1) * DH
        ].astype(F32)
        delta = jnp.sum(product, axis=1, keepdims=True)
        lse = jnp.sum(jnp.where(diagonal, lse_ref[h : h + 1, :], 0.0), axis=1, keepdims=True)
        x = jnp.where(slot == h, lse, x)
        x = jnp.where(slot == heads + h, delta, x)
    high = x.astype(BF16).astype(F32)
    mid = (x - high).astype(BF16).astype(F32)
    low = x - high - mid
    out_ref[:, 2 * width :] = jnp.where(
        term == 0, high, jnp.where(term == 1, mid, jnp.where(term == 2, low, 0.0))
    ).astype(BF16)
    copies[3].wait()


def pack(heads, queries, out_grad, attn_out, logsumexp):
    rows, width = queries.shape
    meta = -(-6 * heads // LANES) * LANES
    return call(
        functools.partial(pack_body, heads),
        local(rows, 2 * width + meta),
        queries,
        out_grad,
        attn_out,
        logsumexp.T,
        hbm=(0, 1, 2, 3),
        scratch=[
            pltpu.VMEM((rows, width), BF16),
            pltpu.VMEM((heads, rows), F32),
            pltpu.SemaphoreType.DMA((4,)),
        ],
        moved=10**6,
    )


def load_body(n, *refs):
    srcs, dsts, sems = refs[:n], refs[n : 2 * n], refs[-1]
    copies = [pltpu.make_async_copy(s, d, sems.at[i]) for i, (s, d) in enumerate(zip(srcs, dsts))]
    for c in copies:
        c.start()
    for c in copies:
        c.wait()


def load(arrays, after):
    n = len(arrays)
    return call(
        functools.partial(load_body, n),
        tuple(local(*a.shape, dtype=a.dtype) for a in arrays),
        *arrays,
        hbm=range(n),
        after=after,
        scratch=[pltpu.SemaphoreType.DMA((n,))],
        moved=2 * sum(a.size * a.dtype.itemsize for a in arrays),
    )


def chunk_body(heads, count_ref, rows_ref, k_ref, v_ref, p_ref, ds_ref, qsum_ref):
    rows, tokens = rows_ref.shape[0], k_ref.shape[0]
    width = k_ref.shape[1]
    live = lax.broadcasted_iota(jnp.int32, (rows, tokens), 1) < count_ref[0]
    terms = rows_ref[:, 2 * width :].astype(F32)
    cut = lambda t: terms[:, t * 2 * heads : (t + 1) * 2 * heads]
    meta = cut(0) + cut(1) + cut(2)
    for h in range(heads):
        cols = slice(h * DH, (h + 1) * DH)
        k = k_ref[:, cols]
        scores = dot(rows_ref[:, cols], k, ((1,), (1,))) * SCALE
        probs = jnp.where(live, jnp.exp(scores - meta[:, h : h + 1]), 0.0)
        p_ref[h] = probs.astype(BF16)
        grads = rows_ref[:, width + h * DH : width + (h + 1) * DH]
        dprobs = dot(grads, v_ref[:, cols], ((1,), (1,)))
        ds = (probs * (dprobs - meta[:, heads + h : heads + h + 1])).astype(BF16)
        ds_ref[h] = ds
        qsum_ref[:, cols] = (dot(ds, k, ((1,), (0,))) * SCALE).astype(qsum_ref.dtype)


def chunk(heads, count, rows, keys, values, after, dtype):
    n, (tokens, width) = rows.shape[0], keys.shape
    return call(
        functools.partial(chunk_body, heads),
        (local(heads, n, tokens), local(heads, n, tokens), local(n, width, dtype=dtype)),
        count,
        rows,
        keys,
        values,
        after=after,
        flops=6 * heads * n * tokens * DH,
        moved=2 * keys.size * 2 + 4 * heads * n * tokens,
    )


def over_rows_body(heads, n, offset, scale, *refs):
    weight_refs, row_refs, out_ref = refs[:n], refs[n : 2 * n], refs[-1]
    for h in range(heads):
        cols = slice(offset + h * DH, offset + (h + 1) * DH)
        w = jnp.concatenate([r[h] for r in weight_refs], axis=0)
        x = jnp.concatenate([r[:, cols] for r in row_refs], axis=0)
        out = dot(w, x, ((0,), (0,)))
        out_ref[:, h * DH : (h + 1) * DH] = (out if scale is None else out * scale).astype(BF16)


def over_rows(weights, chunks, width, offset, scale, after):
    n = len(chunks)
    heads, rows, tokens = weights[0].shape
    return call(
        functools.partial(over_rows_body, heads, n, offset, scale),
        shape(tokens, width),
        *weights,
        *chunks,
        after=after,
        flops=2 * heads * n * rows * tokens * DH,
        moved=2 * heads * n * rows * tokens + 2 * tokens * width,
    )


def gather_sum_body(n, *refs):
    mine, others, keep, outs = refs[0], refs[1:n], refs[n], refs[n + 1 :]
    total = mine[...]
    for r in others:
        total = total + r[...].astype(F32)
    rows = keep.shape[0]
    keep[...] = total[:rows]
    for i, out in enumerate(outs):
        out[...] = total[(i + 1) * rows : (i + 2) * rows].astype(BF16)


def grid_body(n, paired, *refs):
    w_ref, q_ref, out_refs = refs[n], refs[n + 1], refs[n + 2 :]
    total = refs[0][...]
    for r in refs[1:n]:
        total = total + r[...].astype(F32)
    half = total.astype(BF16)
    q_ref[...] = half
    if not paired:
        out_refs[0][...] = dot(half, w_ref[...], ((1,), (1,)))
        return
    me, columns = lax.axis_index("head"), out_refs[0].shape[1]
    for core, out_ref in zip((1 - me, me), out_refs):
        rows = pl.ds(pl.multiple_of(core * columns, columns), columns)
        out_ref[...] = dot(half, w_ref[rows, :], ((1,), (1,)))


def grid_terms(sums, weight, paired, after):
    own, width = sums[0].shape
    outs = (width, width) if paired else (weight.shape[0],)
    return call(
        functools.partial(grid_body, len(sums), paired),
        (shape(own, width),) + tuple(local(own, n, dtype=F32) for n in outs),
        *sums,
        weight,
        after=after,
        flops=2 * own * weight.size,
        moved=2 * weight.size,
    )


def add_body(a_ref, b_ref, out_ref):
    out_ref[...] = (a_ref[...] + b_ref[...]).astype(BF16)


def shifted(i, k, n):
    return i ^ k if n & (n - 1) == 0 else (i + k) % n


def send(x, high, low, k_high, k_low, back=False):
    pairs = []
    for a in range(high):
        for b in range(low):
            there = shifted(a, k_high, high) * low + shifted(b, k_low, low)
            pairs.append((there, a * low + b) if back else (a * low + b, there))
    return lax.ppermute(x, "obs", pairs)


def on_device(obs, head, queries, out_grad, attn_out, logsumexp, keys, values, obs_counts, query_weight):
    own, width = queries.shape
    heads = width // DH
    low = 4 if obs % 4 == 0 else obs
    high = obs // low

    packed = pack(heads, queries, out_grad, attn_out, logsumexp)
    column = [packed] + [send(packed, high, low, k, 0) for k in range(1, high)]
    keys, values, weight = load((keys, values, query_weight), packed)
    column = jnp.concatenate(column, axis=0)
    chunks = [column] + [send(column, high, low, 0, k) for k in range(1, low)]

    probs, dscores, parts = [], [], []
    after = column
    for i, rows in enumerate(chunks):
        p, ds, part = chunk(heads, obs_counts, rows, keys, values, after, BF16 if i else F32)
        after = p
        probs.append(p)
        dscores.append(ds)
        parts.append(send(part, high, low, 0, i, back=True) if i else part)

    value_grad = over_rows(probs, chunks, width, width, None, after)
    sums = call(
        functools.partial(gather_sum_body, low),
        (local(own, width, dtype=F32),) + (local(own, width),) * (high - 1),
        *parts,
        after=[value_grad],
    )
    received = [send(s, high, low, k + 1, 0, back=True) for k, s in enumerate(sums[1:])]
    key_grad = over_rows(dscores, chunks, width, 0, SCALE, sums[0])
    query_grad, *terms = grid_terms([sums[0], *received], weight, head == 2, [key_grad])
    if head == 2:
        other = lax.ppermute(terms[0], "head", [(0, 1), (1, 0)])
        grid_grad = call(add_body, shape(own, width), terms[1], other)
    else:
        grid_grad = lax.psum_scatter(terms[0], "head", scatter_dimension=1, tiled=True).astype(BF16)
    return key_grad, value_grad, query_grad, grid_grad


def solution(mesh):
    both = P("obs", "head")
    return jax.shard_map(
        functools.partial(on_device, mesh.shape["obs"], mesh.shape["head"]),
        mesh=mesh,
        in_specs=(both, both, both, both, both, both, P("obs"), P(None, "head")),
        out_specs=(both,) * 4,
        check_vma=False,
    )
```

```python
import functools
import math

import jax
import jax.numpy as jnp
from jax import lax
from jax.experimental import pallas as pl
from jax.experimental.pallas import tpu as pltpu
from jax.sharding import PartitionSpec as P

DH = 128
LANES = 128
SCALE = 1.0 / math.sqrt(DH)
BF16 = jnp.bfloat16
F32 = jnp.float32


def dot(a, b, contract):
    return lax.dot_general(a, b, (contract, ((), ())), preferred_element_type=F32)


def call(body, out_shape, *args, hbm=(), after=(), done=(), scratch=(), flops=0, moved=0):
    vmem = pl.BlockSpec(memory_space=pltpu.VMEM)
    specs = [
        pl.BlockSpec(memory_space=pltpu.SMEM)
        if a.dtype == jnp.int32
        else pl.BlockSpec(memory_space=pl.ANY) if i in hbm else vmem
        for i, a in enumerate(args)
    ]
    args = [
        a
        if a.dtype == jnp.int32
        else pltpu.with_memory_space_constraint(a, pltpu.HBM if i in hbm else pltpu.VMEM)
        for i, a in enumerate(args)
    ]
    order = [pltpu.with_memory_space_constraint(a, pltpu.VMEM) for a in after]
    order += [pltpu.with_memory_space_constraint(a, pltpu.HBM) for a in done]
    extra = len(order)
    args = order + args
    return pl.pallas_call(
        lambda *refs: body(*refs[extra:]),
        out_shape=out_shape,
        in_specs=[pl.BlockSpec(memory_space=pl.ANY)] * extra + specs,
        out_specs=jax.tree.map(lambda _: vmem, out_shape, is_leaf=lambda x: hasattr(x, "shape")),
        scratch_shapes=scratch,
        compiler_params=pltpu.CompilerParams(vmem_limit_bytes=14 * 2**20),
        cost_estimate=pl.CostEstimate(flops=flops, bytes_accessed=moved, transcendentals=0),
    )(*args)


def shape(*sizes, dtype=BF16):
    return jax.ShapeDtypeStruct(sizes, dtype)


def local(*sizes, dtype=BF16):
    return pltpu.VMEM(sizes, dtype)


def pack_body(heads, q_hbm, g_hbm, a_hbm, lse_hbm, out_ref, a_ref, lse_ref, sems):
    rows, width = a_ref.shape
    copies = [
        pltpu.make_async_copy(src, dst, sems.at[i])
        for i, (src, dst) in enumerate(
            (
                (g_hbm, out_ref.at[:, width : 2 * width]),
                (a_hbm, a_ref),
                (lse_hbm, lse_ref),
                (q_hbm, out_ref.at[:, :width]),
            )
        )
    ]
    for c in copies:
        c.start()
    meta = out_ref.shape[1] - 2 * width
    lane = lax.broadcasted_iota(jnp.int32, (rows, meta), 1)
    slot = lax.rem(lane, 2 * heads)
    term = lane // (2 * heads)
    diagonal = lax.broadcasted_iota(jnp.int32, (rows, rows), 0) == lax.broadcasted_iota(
        jnp.int32, (rows, rows), 1
    )
    x = jnp.zeros((rows, meta), F32)
    for c in copies[:3]:
        c.wait()
    for h in range(heads):
        product = out_ref[:, width + h * DH : width + (h + 1) * DH].astype(F32) * a_ref[
            :, h * DH : (h + 1) * DH
        ].astype(F32)
        delta = jnp.sum(product, axis=1, keepdims=True)
        lse = jnp.sum(jnp.where(diagonal, lse_ref[h : h + 1, :], 0.0), axis=1, keepdims=True)
        x = jnp.where(slot == h, lse, x)
        x = jnp.where(slot == heads + h, delta, x)
    high = x.astype(BF16).astype(F32)
    mid = (x - high).astype(BF16).astype(F32)
    low = x - high - mid
    out_ref[:, 2 * width :] = jnp.where(
        term == 0, high, jnp.where(term == 1, mid, jnp.where(term == 2, low, 0.0))
    ).astype(BF16)
    copies[3].wait()


def pack(heads, queries, out_grad, attn_out, logsumexp):
    rows, width = queries.shape
    meta = -(-6 * heads // LANES) * LANES
    return call(
        functools.partial(pack_body, heads),
        local(rows, 2 * width + meta),
        queries,
        out_grad,
        attn_out,
        logsumexp.T,
        hbm=(0, 1, 2, 3),
        scratch=[
            pltpu.VMEM((rows, width), BF16),
            pltpu.VMEM((heads, rows), F32),
            pltpu.SemaphoreType.DMA((4,)),
        ],
        moved=10**6,
    )


def load_body(n, *refs):
    srcs, dsts, sems = refs[:n], refs[n : 2 * n], refs[-1]
    copies = [pltpu.make_async_copy(s, d, sems.at[i]) for i, (s, d) in enumerate(zip(srcs, dsts))]
    for c in copies:
        c.start()
    for c in copies:
        c.wait()


def join_body(*refs):
    rows = refs[0].shape[0]
    for i, r in enumerate(refs[:-1]):
        refs[-1][i * rows : (i + 1) * rows, :] = r[...]


def join(blocks, after):
    rows, columns = blocks[0].shape
    return call(join_body, local(len(blocks) * rows, columns), *blocks, after=after, moved=10**5)


def load(arrays, after):
    n = len(arrays)
    return call(
        functools.partial(load_body, n),
        tuple(local(*a.shape, dtype=a.dtype) for a in arrays),
        *arrays,
        hbm=range(n),
        after=after,
        scratch=[pltpu.SemaphoreType.DMA((n,))],
        moved=2 * sum(a.size * a.dtype.itemsize for a in arrays),
    )


def chunk_body(heads, count_ref, own_ref, rest_ref, k_ref, v_ref, p_ref, ds_ref, qsum_ref):
    rows, tokens = own_ref.shape[0] + rest_ref.shape[0], k_ref.shape[0]
    width = k_ref.shape[1]
    live = lax.broadcasted_iota(jnp.int32, (rows, tokens), 1) < count_ref[0]
    part = lambda cols: jnp.concatenate([own_ref[:, cols], rest_ref[:, cols]], axis=0)
    terms = part(slice(2 * width, own_ref.shape[1])).astype(F32)
    cut = lambda t: terms[:, t * 2 * heads : (t + 1) * 2 * heads]
    meta = cut(0) + cut(1) + cut(2)

    def products(h):
        cols = slice(h * DH, (h + 1) * DH)
        gcols = slice(width + h * DH, width + (h + 1) * DH)
        scores = dot(part(cols), k_ref[:, cols], ((1,), (1,))) * SCALE
        return scores, dot(part(gcols), v_ref[:, cols], ((1,), (1,)))

    def gradients(h, scores, dprobs):
        probs = jnp.where(live, jnp.exp(scores - meta[:, h : h + 1]), 0.0)
        p_ref[h] = probs.astype(BF16)
        ds = (probs * (dprobs - meta[:, heads + h : heads + h + 1])).astype(BF16)
        ds_ref[h] = ds
        return ds

    def contribution(h, ds):
        cols = slice(h * DH, (h + 1) * DH)
        qsum_ref[:, cols] = (dot(ds, k_ref[:, cols], ((1,), (0,))) * SCALE).astype(qsum_ref.dtype)

    ahead, behind = products(0), None
    for h in range(heads):
        now = ahead
        if h + 1 < heads:
            ahead = products(h + 1)
        ds = gradients(h, *now)
        if h:
            contribution(h - 1, behind)
        behind = ds
    contribution(heads - 1, behind)


def chunk(heads, count, rows, keys, values, after, dtype):
    n, (tokens, width) = sum(r.shape[0] for r in rows), keys.shape
    return call(
        functools.partial(chunk_body, heads),
        (local(heads, n, tokens), local(heads, n, tokens), local(n, width, dtype=dtype)),
        count,
        *rows,
        keys,
        values,
        after=after,
        flops=6 * heads * n * tokens * DH,
        moved=2 * keys.size * 2 + 4 * heads * n * tokens,
    )


def over_rows_body(heads, n, offset, scale, *refs):
    weight_refs, row_refs, out_ref = refs[:n], refs[n:-1], refs[-1]
    for h in range(heads):
        cols = slice(offset + h * DH, offset + (h + 1) * DH)
        w = jnp.concatenate([r[h] for r in weight_refs], axis=0)
        x = jnp.concatenate([r[:, cols] for r in row_refs], axis=0)
        out = dot(w, x, ((0,), (0,)))
        out_ref[:, h * DH : (h + 1) * DH] = (out if scale is None else out * scale).astype(BF16)


def over_rows(weights, chunks, width, offset, scale, after=()):
    n = len(chunks)
    heads, rows, tokens = weights[0].shape
    return call(
        functools.partial(over_rows_body, heads, n, offset, scale),
        shape(tokens, width),
        *weights,
        *(r for rows in chunks for r in rows),
        after=after,
        flops=2 * heads * n * rows * tokens * DH,
        moved=2 * heads * n * rows * tokens + 2 * tokens * width,
    )


def gather_sum_body(n, *refs):
    mine, others, keep, outs = refs[0], refs[1:n], refs[n], refs[n + 1 :]
    total = mine[...]
    for r in others:
        total = total + r[...].astype(F32)
    rows = keep.shape[0]
    keep[...] = total[:rows]
    for i, out in enumerate(outs):
        out[...] = total[(i + 1) * rows : (i + 2) * rows].astype(BF16)


def grid_body(n, paired, *refs):
    w_ref, q_ref, out_refs = refs[n], refs[n + 1], refs[n + 2 :]
    total = refs[0][...]
    for r in refs[1:n]:
        total = total + r[...].astype(F32)
    half = total.astype(BF16)
    q_ref[...] = half
    if not paired:
        out_refs[0][...] = dot(half, w_ref[...], ((1,), (1,)))
        return
    me, columns = lax.axis_index("head"), out_refs[0].shape[1]
    for core, out_ref in zip((1 - me, me), out_refs):
        rows = pl.ds(pl.multiple_of(core * columns, columns), columns)
        out_ref[...] = dot(half, w_ref[rows, :], ((1,), (1,)))


def grid_terms(sums, weight, paired, done):
    own, width = sums[0].shape
    outs = (width, width) if paired else (weight.shape[0],)
    return call(
        functools.partial(grid_body, len(sums), paired),
        (shape(own, width),) + tuple(local(own, n, dtype=F32) for n in outs),
        *sums,
        weight,
        done=done,
        flops=2 * own * weight.size,
        moved=2 * weight.size,
    )


def add_body(a_ref, b_ref, out_ref):
    out_ref[...] = (a_ref[...] + b_ref[...]).astype(BF16)


def shifted(i, k, n):
    return i ^ k if n & (n - 1) == 0 else (i + k) % n


def send(x, high, low, k_high, k_low, back=False):
    pairs = []
    for a in range(high):
        for b in range(low):
            there = shifted(a, k_high, high) * low + shifted(b, k_low, low)
            pairs.append((there, a * low + b) if back else (a * low + b, there))
    return lax.ppermute(x, "obs", pairs)


def on_device(obs, head, queries, out_grad, attn_out, logsumexp, keys, values, obs_counts, query_weight):
    own, width = queries.shape
    heads = width // DH
    low = 4 if obs % 4 == 0 else obs
    high = obs // low

    packed = pack(heads, queries, out_grad, attn_out, logsumexp)
    blocks = [packed] + [send(packed, high, low, 0, k) for k in range(1, low)]
    rest = [send(packed, high, low, k, 0) for k in range(1, high)]
    rest = join(rest, blocks[1:])
    keys, values = load((keys, values), [rest])
    rests = [rest] + [send(rest, high, low, 0, k) for k in range(1, low)]
    chunks = list(zip(blocks, rests))

    probs, dscores, parts = [], [], []
    after = []
    for i, rows in enumerate(chunks):
        p, ds, part = chunk(heads, obs_counts, rows, keys, values, after, BF16 if i else F32)
        after = [p]
        probs.append(p)
        dscores.append(ds)
        parts.append(send(part, high, low, 0, i, back=True) if i else part)

    value_grad = over_rows(probs, chunks, width, width, None)
    sums = call(
        functools.partial(gather_sum_body, low),
        (local(own, width, dtype=F32),) + (local(own, width),) * (high - 1),
        *parts,
        done=[value_grad],
    )
    received = [send(s, high, low, k + 1, 0, back=True) for k, s in enumerate(sums[1:])]
    key_grad = over_rows(dscores, chunks, width, 0, SCALE, [sums[0]])
    query_grad, *terms = grid_terms([sums[0], *received], query_weight, head == 2, [key_grad])
    if head == 2:
        other = lax.ppermute(terms[0], "head", [(0, 1), (1, 0)])
        grid_grad = call(add_body, shape(own, width), terms[1], other)
    else:
        grid_grad = lax.psum_scatter(terms[0], "head", scatter_dimension=1, tiled=True).astype(BF16)
    return key_grad, value_grad, query_grad, grid_grad


def solution(mesh):
    both = P("obs", "head")
    return jax.shard_map(
        functools.partial(on_device, mesh.shape["obs"], mesh.shape["head"]),
        mesh=mesh,
        in_specs=(both, both, both, both, both, both, P("obs"), P(None, "head")),
        out_specs=(both,) * 4,
        check_vma=False,
    )
```

```python
import functools
import math

import jax
import jax.numpy as jnp
from jax import lax
from jax.experimental import pallas as pl
from jax.experimental.pallas import tpu as pltpu
from jax.sharding import PartitionSpec as P

DH = 128
LANES = 128
SUBLANES = 8
SCALE = 1.0 / math.sqrt(DH)
BF16 = jnp.bfloat16
F32 = jnp.float32


def dot(a, b, contract):
    return lax.dot_general(a, b, (contract, ((), ())), preferred_element_type=F32)


def call(body, out_shape, *args, hbm=(), after=(), done=(), scratch=(), flops=0, moved=0):
    vmem = pl.BlockSpec(memory_space=pltpu.VMEM)
    specs = [
        pl.BlockSpec(memory_space=pltpu.SMEM)
        if a.dtype == jnp.int32
        else pl.BlockSpec(memory_space=pl.ANY) if i in hbm else vmem
        for i, a in enumerate(args)
    ]
    args = [
        a
        if a.dtype == jnp.int32
        else pltpu.with_memory_space_constraint(a, pltpu.HBM if i in hbm else pltpu.VMEM)
        for i, a in enumerate(args)
    ]
    order = [pltpu.with_memory_space_constraint(a, pltpu.VMEM) for a in after]
    order += [pltpu.with_memory_space_constraint(a, pltpu.HBM) for a in done]
    extra = len(order)
    args = order + args
    return pl.pallas_call(
        lambda *refs: body(*refs[extra:]),
        out_shape=out_shape,
        in_specs=[pl.BlockSpec(memory_space=pl.ANY)] * extra + specs,
        out_specs=jax.tree.map(lambda _: vmem, out_shape, is_leaf=lambda x: hasattr(x, "shape")),
        scratch_shapes=scratch,
        compiler_params=pltpu.CompilerParams(vmem_limit_bytes=14 * 2**20),
        cost_estimate=pl.CostEstimate(flops=flops, bytes_accessed=moved, transcendentals=0),
    )(*args)


def shape(*sizes, dtype=BF16):
    return jax.ShapeDtypeStruct(sizes, dtype)


def local(*sizes, dtype=BF16):
    return pltpu.VMEM(sizes, dtype)


def pack_body(heads, q_hbm, g_hbm, a_hbm, lse_hbm, out_ref, a_ref, lse_ref, sems):
    rows, width = a_ref.shape
    copies = [
        pltpu.make_async_copy(src, dst, sems.at[i])
        for i, (src, dst) in enumerate(
            (
                (g_hbm, out_ref.at[:, width : 2 * width]),
                (a_hbm, a_ref),
                (lse_hbm, lse_ref),
                (q_hbm, out_ref.at[:, :width]),
            )
        )
    ]
    for c in copies:
        c.start()
    meta = out_ref.shape[1] - 2 * width
    lane = lax.broadcasted_iota(jnp.int32, (rows, meta), 1)
    slot = lax.rem(lane, 2 * heads)
    term = lane // (2 * heads)
    diagonal = lax.broadcasted_iota(jnp.int32, (rows, rows), 0) == lax.broadcasted_iota(
        jnp.int32, (rows, rows), 1
    )
    x = jnp.zeros((rows, meta), F32)
    for c in copies[:3]:
        c.wait()
    for h in range(heads):
        product = out_ref[:, width + h * DH : width + (h + 1) * DH].astype(F32) * a_ref[
            :, h * DH : (h + 1) * DH
        ].astype(F32)
        delta = jnp.sum(product, axis=1, keepdims=True)
        lse = jnp.sum(jnp.where(diagonal, lse_ref[h : h + 1, :], 0.0), axis=1, keepdims=True)
        x = jnp.where(slot == h, lse, x)
        x = jnp.where(slot == heads + h, delta, x)
    high = x.astype(BF16).astype(F32)
    mid = (x - high).astype(BF16).astype(F32)
    low = x - high - mid
    out_ref[:, 2 * width :] = jnp.where(
        term == 0, high, jnp.where(term == 1, mid, jnp.where(term == 2, low, 0.0))
    ).astype(BF16)
    copies[3].wait()


def pack(heads, queries, out_grad, attn_out, logsumexp):
    rows, width = queries.shape
    meta = -(-6 * heads // LANES) * LANES
    return call(
        functools.partial(pack_body, heads),
        local(rows, 2 * width + meta),
        queries,
        out_grad,
        attn_out,
        logsumexp.T,
        hbm=(0, 1, 2, 3),
        scratch=[
            pltpu.VMEM((rows, width), BF16),
            pltpu.VMEM((heads, rows), F32),
            pltpu.SemaphoreType.DMA((4,)),
        ],
        moved=10**6,
    )


def live_body(count_ref, live_ref):
    token = lax.broadcasted_iota(jnp.int32, live_ref.shape, 1)
    live_ref[...] = jnp.where(token < count_ref[0], 1.0, 0.0)


def live_rows(count, tokens):
    return call(live_body, local(SUBLANES, tokens, dtype=F32), count)


def load_body(n, *refs):
    srcs, dsts, sems = refs[:n], refs[n : 2 * n], refs[-1]
    copies = [pltpu.make_async_copy(s, d, sems.at[i]) for i, (s, d) in enumerate(zip(srcs, dsts))]
    for c in copies:
        c.start()
    for c in copies:
        c.wait()


def join_body(*refs):
    rows = refs[0].shape[0]
    for i, r in enumerate(refs[:-1]):
        refs[-1][i * rows : (i + 1) * rows, :] = r[...]


def join(blocks, after):
    rows, columns = blocks[0].shape
    return call(join_body, local(len(blocks) * rows, columns), *blocks, after=after, moved=10**5)


def load(arrays, after):
    n = len(arrays)
    return call(
        functools.partial(load_body, n),
        tuple(local(*a.shape, dtype=a.dtype) for a in arrays),
        *arrays,
        hbm=range(n),
        after=after,
        scratch=[pltpu.SemaphoreType.DMA((n,))],
        moved=2 * sum(a.size * a.dtype.itemsize for a in arrays),
    )


def chunk_body(heads, n, live_ref, *refs):
    row_refs, (k_ref, v_ref, p_ref, ds_ref), part_refs = refs[:n], refs[n : n + 4], refs[n + 4 :]
    width = k_ref.shape[1]
    live = live_ref[:1] > 0.0
    part = lambda cols: jnp.concatenate([r[:, cols] for r in row_refs], axis=0)
    terms = part(slice(2 * width, row_refs[0].shape[1])).astype(F32)
    cut = lambda t: terms[:, t * 2 * heads : (t + 1) * 2 * heads]
    meta = cut(0) + cut(1) + cut(2)

    def products(h):
        cols = slice(h * DH, (h + 1) * DH)
        gcols = slice(width + h * DH, width + (h + 1) * DH)
        scores = dot(part(cols), k_ref[:, cols], ((1,), (1,))) * SCALE
        return scores, dot(part(gcols), v_ref[:, cols], ((1,), (1,)))

    def gradients(h, scores, dprobs):
        probs = jnp.where(live, jnp.exp(scores - meta[:, h : h + 1]), 0.0)
        p_ref[h] = probs.astype(BF16)
        ds = (probs * (dprobs - meta[:, heads + h : heads + h + 1])).astype(BF16)
        ds_ref[h] = ds
        return ds

    def contribution(h, ds):
        cols = slice(h * DH, (h + 1) * DH)
        product = dot(ds, k_ref[:, cols], ((1,), (0,))) * SCALE
        first = 0
        for ref in part_refs:
            ref[:, cols] = product[first : first + ref.shape[0]].astype(ref.dtype)
            first += ref.shape[0]

    ahead, behind = products(0), None
    for h in range(heads):
        now = ahead
        if h + 1 < heads:
            ahead = products(h + 1)
        ds = gradients(h, *now)
        if h:
            contribution(h - 1, behind)
        behind = ds
    contribution(heads - 1, behind)


def chunk(heads, live, groups, keys, values, after, dtype):
    tokens, width = keys.shape
    rows = [r for group in groups for r in group]
    sizes = [sum(r.shape[0] for r in group) for group in groups]
    n = sum(sizes)
    return call(
        functools.partial(chunk_body, heads, len(rows)),
        (local(heads, n, tokens), local(heads, n, tokens))
        + tuple(local(size, width, dtype=dtype) for size in sizes),
        live,
        *rows,
        keys,
        values,
        after=after,
        flops=6 * heads * n * tokens * DH,
        moved=2 * keys.size * 2 + 4 * heads * n * tokens,
    )


def over_rows_body(heads, n, offset, scale, *refs):
    weight_refs, row_refs, out_ref = refs[:n], refs[n:-1], refs[-1]
    for h in range(heads):
        cols = slice(offset + h * DH, offset + (h + 1) * DH)
        w = jnp.concatenate([r[h] for r in weight_refs], axis=0)
        x = jnp.concatenate([r[:, cols] for r in row_refs], axis=0)
        out = dot(w, x, ((0,), (0,)))
        out_ref[:, h * DH : (h + 1) * DH] = (out if scale is None else out * scale).astype(BF16)


def over_rows(weights, rows, width, offset, scale, after=()):
    heads, _, tokens = weights[0].shape
    total = sum(r.shape[0] for r in rows)
    return call(
        functools.partial(over_rows_body, heads, len(weights), offset, scale),
        shape(tokens, width),
        *weights,
        *rows,
        after=after,
        flops=2 * heads * total * tokens * DH,
        moved=2 * heads * total * tokens + 2 * tokens * width,
    )


def gather_sum_body(n, *refs):
    mine, others, keep, outs = refs[0], refs[1:n], refs[n], refs[n + 1 :]
    total = mine[...]
    for r in others:
        total = total + r[...].astype(F32)
    rows = keep.shape[0]
    keep[...] = total[:rows]
    for i, out in enumerate(outs):
        out[...] = total[(i + 1) * rows : (i + 2) * rows].astype(BF16)


def grid_body(n, half, *refs):
    w_ref, outs = refs[n], refs[n + 1 :]
    total = refs[0][...].astype(F32)
    for r in refs[1:n]:
        total = total + r[...].astype(F32)
    rounded = total.astype(BF16)
    if n > 1:
        outs[0][...] = rounded
    columns = outs[-1].shape[1]
    first = 0
    if half is not None:
        me = lax.axis_index("head")
        first = pl.multiple_of((1 - me if half else me) * columns, columns)
    outs[-1][...] = dot(rounded, w_ref[pl.ds(first, columns), :], ((1,), (1,)))


def grid_term(terms, weight, half, columns, done):
    own, width = terms[0].shape
    return call(
        functools.partial(grid_body, len(terms), half),
        ((local(own, width),) if len(terms) > 1 else ()) + (local(own, columns, dtype=F32),),
        *terms,
        weight,
        done=done,
        flops=2 * own * columns * width,
        moved=2 * columns * width,
    )


def last_body(a_ref, b_ref, rounded_ref, grid_ref, query_ref):
    grid_ref[...] = (a_ref[...] + b_ref[...]).astype(BF16)
    query_ref[...] = rounded_ref[...]


def shifted(i, k, n):
    return i ^ k if n & (n - 1) == 0 else (i + k) % n


def send(x, high, low, k_high, k_low, back=False):
    pairs = []
    for a in range(high):
        for b in range(low):
            there = shifted(a, k_high, high) * low + shifted(b, k_low, low)
            pairs.append((there, a * low + b) if back else (a * low + b, there))
    return lax.ppermute(x, "obs", pairs)


def on_device(obs, head, queries, out_grad, attn_out, logsumexp, keys, values, obs_counts, query_weight):
    own, width = queries.shape
    heads = width // DH
    low = 4 if obs % 4 == 0 else obs
    high = obs // low

    packed = pack(heads, queries, out_grad, attn_out, logsumexp)
    plane = 3 if low == 4 else low
    across = [send(packed, high, low, 0, k) for k in range(plane, low)]
    column = [packed] + [send(packed, high, low, k, 0) for k in range(1, high)]
    live = live_rows(obs_counts, keys.shape[0])
    keys, values = load((keys, values), [packed])
    column = join(column, [keys, live, *across])
    chunks = [[send(column, high, low, 0, k)] for k in range(1, plane)]
    chunks += [[x] + [send(x, high, low, k, 0) for k in range(1, high)] for x in across]

    probs, dscores, parts, rows = [], [], [], []
    for groups, dtype in [(chunks[:2], BF16)] + [([c], BF16) for c in chunks[2:]] + [([[column]], F32)]:
        p, ds, *contributions = chunk(heads, live, groups, keys, values, probs[-1:], dtype)
        probs.append(p)
        dscores.append(ds)
        rows += [r for group in groups for r in group]
        parts += contributions
    parts = [parts[-1]] + [
        send(x, high, low, 0, k + 1, back=True) for k, x in enumerate(parts[:-1])
    ]

    value_grad = over_rows(probs, rows, width, width, None)
    sums = call(
        functools.partial(gather_sum_body, low),
        (local(own, width, dtype=F32),) + (local(own, width),) * (high - 1),
        *parts,
        done=[value_grad],
    )
    received = [send(s, high, low, k + 1, 0, back=True) for k, s in enumerate(sums[1:])]
    key_grad = over_rows(dscores, rows, width, 0, SCALE, [sums[0]])
    terms = [sums[0], *received]
    if head == 2:
        rounded, other = grid_term(terms, query_weight, 1, width, [key_grad])
        other = lax.ppermute(other, "head", [(0, 1), (1, 0)])
        (mine,) = grid_term([rounded], query_weight, 0, width, [])
        grid_grad, query_grad = call(last_body, (shape(own, width),) * 2, mine, other, rounded)
    else:
        query_grad, part = grid_term(terms, query_weight, None, query_weight.shape[0], [key_grad])
        grid_grad = lax.psum_scatter(part, "head", scatter_dimension=1, tiled=True).astype(BF16)
    return key_grad, value_grad, query_grad, grid_grad


def solution(mesh):
    both = P("obs", "head")
    return jax.shard_map(
        functools.partial(on_device, mesh.shape["obs"], mesh.shape["head"]),
        mesh=mesh,
        in_specs=(both, both, both, both, both, both, P("obs"), P(None, "head")),
        out_specs=(both,) * 4,
        check_vma=False,
    )
```

```python
import functools
import math

import jax
import jax.numpy as jnp
from jax import lax
from jax.experimental import pallas as pl
from jax.experimental.pallas import tpu as pltpu
from jax.sharding import PartitionSpec as P

DH = 128
LANES = 128
SUBLANES = 8
SCALE = 1.0 / math.sqrt(DH)
BF16 = jnp.bfloat16
F32 = jnp.float32


def dot(a, b, contract):
    return lax.dot_general(a, b, (contract, ((), ())), preferred_element_type=F32)


def call(body, out_shape, *args, hbm=(), after=(), done=(), scratch=(), flops=0, moved=0):
    vmem = pl.BlockSpec(memory_space=pltpu.VMEM)
    specs = [
        pl.BlockSpec(memory_space=pltpu.SMEM)
        if a.dtype == jnp.int32
        else pl.BlockSpec(memory_space=pl.ANY) if i in hbm else vmem
        for i, a in enumerate(args)
    ]
    args = [
        a
        if a.dtype == jnp.int32
        else pltpu.with_memory_space_constraint(a, pltpu.HBM if i in hbm else pltpu.VMEM)
        for i, a in enumerate(args)
    ]
    order = [pltpu.with_memory_space_constraint(a, pltpu.VMEM) for a in after]
    order += [pltpu.with_memory_space_constraint(a, pltpu.HBM) for a in done]
    extra = len(order)
    args = order + args
    return pl.pallas_call(
        lambda *refs: body(*refs[extra:]),
        out_shape=out_shape,
        in_specs=[pl.BlockSpec(memory_space=pl.ANY)] * extra + specs,
        out_specs=jax.tree.map(lambda _: vmem, out_shape, is_leaf=lambda x: hasattr(x, "shape")),
        scratch_shapes=scratch,
        compiler_params=pltpu.CompilerParams(vmem_limit_bytes=14 * 2**20),
        cost_estimate=pl.CostEstimate(flops=flops, bytes_accessed=moved, transcendentals=0),
    )(*args)


def shape(*sizes, dtype=BF16):
    return jax.ShapeDtypeStruct(sizes, dtype)


def local(*sizes, dtype=BF16):
    return pltpu.VMEM(sizes, dtype)


def pack_body(heads, q_hbm, g_hbm, a_hbm, lse_hbm, out_ref, a_ref, lse_ref, sems):
    rows, width = a_ref.shape
    copies = [
        pltpu.make_async_copy(src, dst, sems.at[i])
        for i, (src, dst) in enumerate(
            (
                (g_hbm, out_ref.at[:, width : 2 * width]),
                (a_hbm, a_ref),
                (lse_hbm, lse_ref),
                (q_hbm, out_ref.at[:, :width]),
            )
        )
    ]
    for c in copies:
        c.start()
    meta = out_ref.shape[1] - 2 * width
    lane = lax.broadcasted_iota(jnp.int32, (rows, meta), 1)
    slot = lax.rem(lane, 2 * heads)
    term = lane // (2 * heads)
    diagonal = lax.broadcasted_iota(jnp.int32, (rows, rows), 0) == lax.broadcasted_iota(
        jnp.int32, (rows, rows), 1
    )
    x = jnp.zeros((rows, meta), F32)
    for c in copies[:3]:
        c.wait()
    for h in range(heads):
        product = out_ref[:, width + h * DH : width + (h + 1) * DH].astype(F32) * a_ref[
            :, h * DH : (h + 1) * DH
        ].astype(F32)
        delta = jnp.sum(product, axis=1, keepdims=True)
        lse = jnp.sum(jnp.where(diagonal, lse_ref[h : h + 1, :], 0.0), axis=1, keepdims=True)
        x = jnp.where(slot == h, lse, x)
        x = jnp.where(slot == heads + h, delta, x)
    high = x.astype(BF16).astype(F32)
    mid = (x - high).astype(BF16).astype(F32)
    low = x - high - mid
    out_ref[:, 2 * width :] = jnp.where(
        term == 0, high, jnp.where(term == 1, mid, jnp.where(term == 2, low, 0.0))
    ).astype(BF16)
    copies[3].wait()


def pack(heads, queries, out_grad, attn_out, logsumexp):
    rows, width = queries.shape
    meta = -(-6 * heads // LANES) * LANES
    return call(
        functools.partial(pack_body, heads),
        local(rows, 2 * width + meta),
        queries,
        out_grad,
        attn_out,
        logsumexp.T,
        hbm=(0, 1, 2, 3),
        scratch=[
            pltpu.VMEM((rows, width), BF16),
            pltpu.VMEM((heads, rows), F32),
            pltpu.SemaphoreType.DMA((4,)),
        ],
        moved=10**6,
    )


def live_body(count_ref, live_ref):
    token = lax.broadcasted_iota(jnp.int32, live_ref.shape, 1)
    live_ref[...] = jnp.where(token < count_ref[0], 1.0, 0.0)


def live_rows(count, tokens):
    return call(live_body, local(SUBLANES, tokens, dtype=F32), count)


def load_body(n, *refs):
    srcs, dsts, sems = refs[:n], refs[n : 2 * n], refs[-1]
    copies = [pltpu.make_async_copy(s, d, sems.at[i]) for i, (s, d) in enumerate(zip(srcs, dsts))]
    for c in copies:
        c.start()
    for c in copies:
        c.wait()


def join_body(*refs):
    rows = refs[0].shape[0]
    for i, r in enumerate(refs[:-1]):
        refs[-1][i * rows : (i + 1) * rows, :] = r[...]


def join(blocks, after):
    rows, columns = blocks[0].shape
    return call(join_body, local(len(blocks) * rows, columns), *blocks, after=after, moved=10**5)


def load(arrays, after):
    n = len(arrays)
    return call(
        functools.partial(load_body, n),
        tuple(local(*a.shape, dtype=a.dtype) for a in arrays),
        *arrays,
        hbm=range(n),
        after=after,
        scratch=[pltpu.SemaphoreType.DMA((n,))],
        moved=2 * sum(a.size * a.dtype.itemsize for a in arrays),
    )


def chunk_body(heads, n, live_ref, *refs):
    row_refs, (k_ref, v_ref, p_ref, ds_ref), part_refs = refs[:n], refs[n : n + 4], refs[n + 4 :]
    width = k_ref.shape[1]
    live = live_ref[:1] > 0.0
    part = lambda cols: jnp.concatenate([r[:, cols] for r in row_refs], axis=0)
    terms = part(slice(2 * width, row_refs[0].shape[1])).astype(F32)
    cut = lambda t: terms[:, t * 2 * heads : (t + 1) * 2 * heads]
    meta = cut(0) + cut(1) + cut(2)

    def products(h):
        cols = slice(h * DH, (h + 1) * DH)
        gcols = slice(width + h * DH, width + (h + 1) * DH)
        scores = dot(part(cols), k_ref[:, cols], ((1,), (1,))) * SCALE
        return scores, dot(part(gcols), v_ref[:, cols], ((1,), (1,)))

    def gradients(h, scores, dprobs):
        probs = jnp.where(live, jnp.exp(scores - meta[:, h : h + 1]), 0.0)
        p_ref[h] = probs.astype(BF16)
        ds = (probs * (dprobs - meta[:, heads + h : heads + h + 1])).astype(BF16)
        ds_ref[h] = ds
        return ds

    def contribution(h, ds):
        cols = slice(h * DH, (h + 1) * DH)
        product = dot(ds, k_ref[:, cols], ((1,), (0,))) * SCALE
        first = 0
        for ref in part_refs:
            ref[:, cols] = product[first : first + ref.shape[0]].astype(ref.dtype)
            first += ref.shape[0]

    ahead, behind = products(0), None
    for h in range(heads):
        now = ahead
        if h + 1 < heads:
            ahead = products(h + 1)
        ds = gradients(h, *now)
        if h:
            contribution(h - 1, behind)
        behind = ds
    contribution(heads - 1, behind)


def chunk(heads, live, groups, keys, values, after, dtype):
    tokens, width = keys.shape
    rows = [r for group in groups for r in group]
    sizes = [sum(r.shape[0] for r in group) for group in groups]
    n = sum(sizes)
    return call(
        functools.partial(chunk_body, heads, len(rows)),
        (local(heads, n, tokens), local(heads, n, tokens))
        + tuple(local(size, width, dtype=dtype) for size in sizes),
        live,
        *rows,
        keys,
        values,
        after=after,
        flops=6 * heads * n * tokens * DH,
        moved=2 * keys.size * 2 + 4 * heads * n * tokens,
    )


def over_rows_body(heads, n, offset, scale, *refs):
    weight_refs, row_refs, out_ref = refs[:n], refs[n:-1], refs[-1]
    for h in range(heads):
        cols = slice(offset + h * DH, offset + (h + 1) * DH)
        w = jnp.concatenate([r[h] for r in weight_refs], axis=0)
        x = jnp.concatenate([r[:, cols] for r in row_refs], axis=0)
        out = dot(w, x, ((0,), (0,)))
        out_ref[:, h * DH : (h + 1) * DH] = (out if scale is None else out * scale).astype(BF16)


def over_rows(weights, rows, width, offset, scale, after=()):
    heads, _, tokens = weights[0].shape
    total = sum(r.shape[0] for r in rows)
    return call(
        functools.partial(over_rows_body, heads, len(weights), offset, scale),
        shape(tokens, width),
        *weights,
        *rows,
        after=after,
        flops=2 * heads * total * tokens * DH,
        moved=2 * heads * total * tokens + 2 * tokens * width,
    )


def gather_sum_body(n, *refs):
    mine, others, keep, outs = refs[0], refs[1:n], refs[n], refs[n + 1 :]
    total = mine[...]
    for r in others:
        total = total + r[...].astype(F32)
    rows = keep.shape[0]
    keep[...] = total[:rows]
    for i, out in enumerate(outs):
        out[...] = total[(i + 1) * rows : (i + 2) * rows].astype(BF16)


def grid_body(n, half, *refs):
    w_ref, outs = refs[n], refs[n + 1 :]
    total = refs[0][...].astype(F32)
    for r in refs[1:n]:
        total = total + r[...].astype(F32)
    rounded = total.astype(BF16)
    if n > 1:
        outs[0][...] = rounded
    columns = outs[-1].shape[1]
    first = 0
    if half is not None:
        me = lax.axis_index("head")
        first = pl.multiple_of((1 - me if half else me) * columns, columns)
    outs[-1][...] = dot(rounded, w_ref[pl.ds(first, columns), :], ((1,), (1,)))


def grid_term(terms, weight, half, columns, done):
    own, width = terms[0].shape
    return call(
        functools.partial(grid_body, len(terms), half),
        ((local(own, width),) if len(terms) > 1 else ()) + (local(own, columns, dtype=F32),),
        *terms,
        weight,
        done=done,
        flops=2 * own * columns * width,
        moved=2 * columns * width,
    )


def last_body(a_ref, b_ref, rounded_ref, grid_ref, query_ref):
    grid_ref[...] = (a_ref[...] + b_ref[...]).astype(BF16)
    query_ref[...] = rounded_ref[...]


def shifted(i, k, n):
    return i ^ k if n & (n - 1) == 0 else (i + k) % n


def send(x, high, low, k_high, k_low, back=False):
    pairs = []
    for a in range(high):
        for b in range(low):
            there = shifted(a, k_high, high) * low + shifted(b, k_low, low)
            pairs.append((there, a * low + b) if back else (a * low + b, there))
    return lax.ppermute(x, "obs", pairs)


def on_device(obs, head, queries, out_grad, attn_out, logsumexp, keys, values, obs_counts, query_weight):
    own, width = queries.shape
    heads = width // DH
    low = 4 if obs % 4 == 0 else obs
    high = obs // low

    packed = pack(heads, queries, out_grad, attn_out, logsumexp)
    plane = 3 if low == 4 else low
    across = [send(packed, high, low, 0, k) for k in range(plane, low)]
    column = [packed] + [send(packed, high, low, k, 0) for k in range(1, high)]
    live = live_rows(obs_counts, keys.shape[0])
    keys, values = load((keys, values), [packed])
    column = join(column, [keys, live, *across])
    chunks = [[send(column, high, low, 0, k)] for k in range(1, plane)]
    chunks += [[x] + [send(x, high, low, k, 0) for k in range(1, high)] for x in across]

    probs, dscores, parts, rows = [], [], [], []
    for groups, dtype in [(chunks[:2], BF16)] + [([c], BF16) for c in chunks[2:]] + [([[column]], F32)]:
        p, ds, *contributions = chunk(heads, live, groups, keys, values, probs[-1:], dtype)
        probs.append(p)
        dscores.append(ds)
        rows += [r for group in groups for r in group]
        parts += contributions
    parts = [parts[-1]] + [
        send(x, high, low, 0, k + 1, back=True) for k, x in enumerate(parts[:-1])
    ]

    value_grad = over_rows(probs, rows, width, width, None)
    sums = call(
        functools.partial(gather_sum_body, low),
        (local(own, width, dtype=F32),) + (local(own, width),) * (high - 1),
        *parts,
        done=[value_grad],
    )
    received = [send(s, high, low, k + 1, 0, back=True) for k, s in enumerate(sums[1:])]
    key_grad = over_rows(dscores, rows, width, 0, SCALE, [sums[0]])
    terms = [sums[0], *(received[i] for i in (1, 2, 0))]
    if head == 2:
        rounded, other = grid_term(terms, query_weight, 1, width, [key_grad])
        other = lax.ppermute(other, "head", [(0, 1), (1, 0)])
        (mine,) = grid_term([rounded], query_weight, 0, width, [])
        grid_grad, query_grad = call(last_body, (shape(own, width),) * 2, mine, other, rounded)
    else:
        query_grad, part = grid_term(terms, query_weight, None, query_weight.shape[0], [key_grad])
        grid_grad = lax.psum_scatter(part, "head", scatter_dimension=1, tiled=True).astype(BF16)
    return key_grad, value_grad, query_grad, grid_grad


def solution(mesh):
    both = P("obs", "head")
    return jax.shard_map(
        functools.partial(on_device, mesh.shape["obs"], mesh.shape["head"]),
        mesh=mesh,
        in_specs=(both, both, both, both, both, both, P("obs"), P(None, "head")),
        out_specs=(both,) * 4,
        check_vma=False,
    )
```

```python
import functools
import math

import jax
import jax.numpy as jnp
from jax import lax
from jax.experimental import pallas as pl
from jax.experimental.pallas import tpu as pltpu
from jax.sharding import PartitionSpec as P

DH = 128
LANES = 128
SUBLANES = 8
SCALE = 1.0 / math.sqrt(DH)
BF16 = jnp.bfloat16
F32 = jnp.float32


def dot(a, b, contract):
    return lax.dot_general(a, b, (contract, ((), ())), preferred_element_type=F32)


def call(body, out_shape, *args, hbm=(), after=(), done=(), scratch=(), flops=0, moved=0):
    vmem = pl.BlockSpec(memory_space=pltpu.VMEM)
    specs = [
        pl.BlockSpec(memory_space=pltpu.SMEM)
        if a.dtype == jnp.int32
        else pl.BlockSpec(memory_space=pl.ANY) if i in hbm else vmem
        for i, a in enumerate(args)
    ]
    args = [
        a
        if a.dtype == jnp.int32
        else pltpu.with_memory_space_constraint(a, pltpu.HBM if i in hbm else pltpu.VMEM)
        for i, a in enumerate(args)
    ]
    order = [pltpu.with_memory_space_constraint(a, pltpu.VMEM) for a in after]
    order += [pltpu.with_memory_space_constraint(a, pltpu.HBM) for a in done]
    extra = len(order)
    args = order + args
    return pl.pallas_call(
        lambda *refs: body(*refs[extra:]),
        out_shape=out_shape,
        in_specs=[pl.BlockSpec(memory_space=pl.ANY)] * extra + specs,
        out_specs=jax.tree.map(lambda _: vmem, out_shape, is_leaf=lambda x: hasattr(x, "shape")),
        scratch_shapes=scratch,
        compiler_params=pltpu.CompilerParams(vmem_limit_bytes=14 * 2**20),
        cost_estimate=pl.CostEstimate(flops=flops, bytes_accessed=moved, transcendentals=0),
    )(*args)


def shape(*sizes, dtype=BF16):
    return jax.ShapeDtypeStruct(sizes, dtype)


def local(*sizes, dtype=BF16):
    return pltpu.VMEM(sizes, dtype)


def pack_body(heads, q_hbm, g_hbm, a_hbm, lse_hbm, out_ref, a_ref, lse_ref, sems):
    rows, width = a_ref.shape
    copies = [
        pltpu.make_async_copy(src, dst, sems.at[i])
        for i, (src, dst) in enumerate(
            (
                (g_hbm, out_ref.at[:, width : 2 * width]),
                (a_hbm, a_ref),
                (lse_hbm, lse_ref),
                (q_hbm, out_ref.at[:, :width]),
            )
        )
    ]
    for c in copies:
        c.start()
    meta = out_ref.shape[1] - 2 * width
    lane = lax.broadcasted_iota(jnp.int32, (rows, meta), 1)
    slot = lax.rem(lane, 2 * heads)
    term = lane // (2 * heads)
    diagonal = lax.broadcasted_iota(jnp.int32, (rows, rows), 0) == lax.broadcasted_iota(
        jnp.int32, (rows, rows), 1
    )
    x = jnp.zeros((rows, meta), F32)
    for c in copies[:3]:
        c.wait()
    for h in range(heads):
        product = out_ref[:, width + h * DH : width + (h + 1) * DH].astype(F32) * a_ref[
            :, h * DH : (h + 1) * DH
        ].astype(F32)
        delta = jnp.sum(product, axis=1, keepdims=True)
        lse = jnp.sum(jnp.where(diagonal, lse_ref[h : h + 1, :], 0.0), axis=1, keepdims=True)
        x = jnp.where(slot == h, lse, x)
        x = jnp.where(slot == heads + h, delta, x)
    high = x.astype(BF16).astype(F32)
    mid = (x - high).astype(BF16).astype(F32)
    low = x - high - mid
    out_ref[:, 2 * width :] = jnp.where(
        term == 0, high, jnp.where(term == 1, mid, jnp.where(term == 2, low, 0.0))
    ).astype(BF16)
    copies[3].wait()


def pack(heads, queries, out_grad, attn_out, logsumexp):
    rows, width = queries.shape
    meta = -(-6 * heads // LANES) * LANES
    return call(
        functools.partial(pack_body, heads),
        local(rows, 2 * width + meta),
        queries,
        out_grad,
        attn_out,
        logsumexp.T,
        hbm=(0, 1, 2, 3),
        scratch=[
            pltpu.VMEM((rows, width), BF16),
            pltpu.VMEM((heads, rows), F32),
            pltpu.SemaphoreType.DMA((4,)),
        ],
        moved=10**6,
    )


def live_body(count_ref, live_ref):
    token = lax.broadcasted_iota(jnp.int32, live_ref.shape, 1)
    live_ref[...] = jnp.where(token < count_ref[0], 1.0, 0.0)


def live_rows(count, tokens):
    return call(live_body, local(SUBLANES, tokens, dtype=F32), count)


def load_body(n, *refs):
    srcs, dsts, sems = refs[:n], refs[n : 2 * n], refs[-1]
    copies = [pltpu.make_async_copy(s, d, sems.at[i]) for i, (s, d) in enumerate(zip(srcs, dsts))]
    for c in copies:
        c.start()
    for c in copies:
        c.wait()


def join_body(*refs):
    rows = refs[0].shape[0]
    for i, r in enumerate(refs[-2::-1]):
        refs[-1][i * rows : (i + 1) * rows, :] = r[...]


def join(blocks, after):
    rows, columns = blocks[0].shape
    return call(join_body, local(len(blocks) * rows, columns), *blocks[::-1], after=after, moved=10**5)


def load(arrays, after):
    n = len(arrays)
    return call(
        functools.partial(load_body, n),
        tuple(local(*a.shape, dtype=a.dtype) for a in arrays),
        *arrays,
        hbm=range(n),
        after=after,
        scratch=[pltpu.SemaphoreType.DMA((n,))],
        moved=2 * sum(a.size * a.dtype.itemsize for a in arrays),
    )


def chunk_body(heads, n, live_ref, *refs):
    row_refs, (k_ref, v_ref, p_ref, ds_ref), part_refs = refs[:n], refs[n : n + 4], refs[n + 4 :]
    width = k_ref.shape[1]
    live = live_ref[:1] > 0.0
    part = lambda cols: jnp.concatenate([r[:, cols] for r in row_refs], axis=0)
    terms = part(slice(2 * width, row_refs[0].shape[1])).astype(F32)
    cut = lambda t: terms[:, t * 2 * heads : (t + 1) * 2 * heads]
    meta = cut(0) + cut(1) + cut(2)

    def products(h):
        cols = slice(h * DH, (h + 1) * DH)
        gcols = slice(width + h * DH, width + (h + 1) * DH)
        scores = dot(part(cols), k_ref[:, cols], ((1,), (1,))) * SCALE
        return scores, dot(part(gcols), v_ref[:, cols], ((1,), (1,)))

    def gradients(h, scores, dprobs):
        probs = jnp.where(live, jnp.exp(scores - meta[:, h : h + 1]), 0.0)
        p_ref[h] = probs.astype(BF16)
        ds = (probs * (dprobs - meta[:, heads + h : heads + h + 1])).astype(BF16)
        ds_ref[h] = ds
        return ds

    def contribution(h, ds):
        cols = slice(h * DH, (h + 1) * DH)
        product = dot(ds, k_ref[:, cols], ((1,), (0,))) * SCALE
        first = 0
        for ref in part_refs:
            ref[:, cols] = product[first : first + ref.shape[0]].astype(ref.dtype)
            first += ref.shape[0]

    ahead, behind = products(0), None
    for h in range(heads):
        now = ahead
        if h + 1 < heads:
            ahead = products(h + 1)
        ds = gradients(h, *now)
        if h:
            contribution(h - 1, behind)
        behind = ds
    contribution(heads - 1, behind)


def chunk(heads, live, groups, keys, values, after, dtype):
    tokens, width = keys.shape
    rows = [r for group in groups for r in group]
    sizes = [sum(r.shape[0] for r in group) for group in groups]
    n = sum(sizes)
    return call(
        functools.partial(chunk_body, heads, len(rows)),
        (local(heads, n, tokens), local(heads, n, tokens))
        + tuple(local(size, width, dtype=dtype) for size in sizes),
        live,
        *rows,
        keys,
        values,
        after=after,
        flops=6 * heads * n * tokens * DH,
        moved=2 * keys.size * 2 + 4 * heads * n * tokens,
    )


def over_rows_body(heads, n, offset, scale, *refs):
    weight_refs, row_refs, out_ref = refs[:n], refs[n:-1], refs[-1]
    for h in range(heads):
        cols = slice(offset + h * DH, offset + (h + 1) * DH)
        w = jnp.concatenate([r[h] for r in weight_refs], axis=0)
        x = jnp.concatenate([r[:, cols] for r in row_refs], axis=0)
        out = dot(w, x, ((0,), (0,)))
        out_ref[:, h * DH : (h + 1) * DH] = (out if scale is None else out * scale).astype(BF16)


def over_rows(weights, rows, width, offset, scale, after=()):
    heads, _, tokens = weights[0].shape
    total = sum(r.shape[0] for r in rows)
    return call(
        functools.partial(over_rows_body, heads, len(weights), offset, scale),
        shape(tokens, width),
        *weights,
        *rows,
        after=after,
        flops=2 * heads * total * tokens * DH,
        moved=2 * heads * total * tokens + 2 * tokens * width,
    )


def gather_sum_body(n, *refs):
    mine, others, keep, outs = refs[0], refs[1:n], refs[n], refs[n + 1 :]
    total = mine[...]
    for r in others:
        total = total + r[...].astype(F32)
    rows = keep.shape[0]
    keep[...] = total[:rows]
    for i, out in enumerate(outs):
        out[...] = total[(i + 1) * rows : (i + 2) * rows].astype(BF16)


def grid_body(n, half, *refs):
    w_ref, outs = refs[n], refs[n + 1 :]
    total = refs[0][...].astype(F32)
    for r in refs[1:n]:
        total = total + r[...].astype(F32)
    rounded = total.astype(BF16)
    if n > 1:
        outs[0][...] = rounded
    columns = outs[-1].shape[1]
    first = 0
    if half is not None:
        me = lax.axis_index("head")
        first = pl.multiple_of((1 - me if half else me) * columns, columns)
    outs[-1][...] = dot(rounded, w_ref[pl.ds(first, columns), :], ((1,), (1,)))


def grid_term(terms, weight, half, columns, done):
    own, width = terms[0].shape
    return call(
        functools.partial(grid_body, len(terms), half),
        ((local(own, width),) if len(terms) > 1 else ()) + (local(own, columns, dtype=F32),),
        *terms,
        weight,
        done=done,
        flops=2 * own * columns * width,
        moved=2 * columns * width,
    )


def last_body(a_ref, b_ref, rounded_ref, grid_ref, query_ref):
    grid_ref[...] = (a_ref[...] + b_ref[...]).astype(BF16)
    query_ref[...] = rounded_ref[...]


def shifted(i, k, n):
    return i ^ k if n & (n - 1) == 0 else (i + k) % n


def send(x, high, low, k_high, k_low, back=False):
    pairs = []
    for a in range(high):
        for b in range(low):
            there = (a + k_high) % high * low + shifted(b, k_low, low)
            pairs.append((there, a * low + b) if back else (a * low + b, there))
    return lax.ppermute(x, "obs", pairs)


def on_device(obs, head, queries, out_grad, attn_out, logsumexp, keys, values, obs_counts, query_weight):
    own, width = queries.shape
    heads = width // DH
    low = 4 if obs % 4 == 0 else obs
    high = obs // low

    packed = pack(heads, queries, out_grad, attn_out, logsumexp)
    plane = 3 if low == 4 else low
    across = [send(packed, high, low, 0, k) for k in range(plane, low)]
    column = [packed] + [send(packed, high, low, k, 0) for k in range(1, high)]
    live = live_rows(obs_counts, keys.shape[0])
    keys, values = load((keys, values), [packed])
    column = join(column, [keys, live, *across])
    chunks = [[send(column, high, low, 0, k)] for k in range(1, plane)]
    chunks += [[x] + [send(x, high, low, k, 0) for k in range(1, high)] for x in across]

    probs, dscores, parts, rows = [], [], [], []
    for groups, dtype in [(chunks[:2], BF16)] + [([c], BF16) for c in chunks[2:]] + [([[column]], F32)]:
        p, ds, *contributions = chunk(heads, live, groups, keys, values, probs[-1:], dtype)
        probs.append(p)
        dscores.append(ds)
        rows += [r for group in groups for r in group]
        parts += contributions
    parts = [parts[-1]] + [
        send(x, high, low, 0, k + 1, back=True) for k, x in enumerate(parts[:-1])
    ]

    value_grad = over_rows(probs, rows, width, width, None)
    sums = call(
        functools.partial(gather_sum_body, low),
        (local(own, width, dtype=F32),) + (local(own, width),) * (high - 1),
        *parts,
        done=[value_grad],
    )
    received = [send(s, high, low, k + 1, 0, back=True) for k, s in enumerate(sums[1:])]
    key_grad = over_rows(dscores, rows, width, 0, SCALE, [sums[0]])
    terms = [sums[0], *received[::-1]]
    if head == 2:
        rounded, other = grid_term(terms, query_weight, 1, width, [key_grad])
        other = lax.ppermute(other, "head", [(0, 1), (1, 0)])
        (mine,) = grid_term([rounded], query_weight, 0, width, [])
        grid_grad, query_grad = call(last_body, (shape(own, width),) * 2, mine, other, rounded)
    else:
        query_grad, part = grid_term(terms, query_weight, None, query_weight.shape[0], [key_grad])
        grid_grad = lax.psum_scatter(part, "head", scatter_dimension=1, tiled=True).astype(BF16)
    return key_grad, value_grad, query_grad, grid_grad


def solution(mesh):
    both = P("obs", "head")
    return jax.shard_map(
        functools.partial(on_device, mesh.shape["obs"], mesh.shape["head"]),
        mesh=mesh,
        in_specs=(both, both, both, both, both, both, P("obs"), P(None, "head")),
        out_specs=(both,) * 4,
        check_vma=False,
    )
```
